128 devices in a mesh: span: 4 (over z_lo, core), cp: 32 (over y, z_hi, x).
Axes of the slice: x: 4, y: 4, z: 4 (z_hi: 2, z_lo: 2; z = z_hi * 2 + z_lo), core: 2. Of those that a mesh axis runs over, the one named last changes fastest.
Arguments:
- queries: bfloat16 [4, 3072, 4096], P('span', 'cp'), may hold values from -12 to 12
- keys: bfloat16 [4, 3072, 4096], P('span', 'cp'), may hold values from -40 to 40
- values: bfloat16 [4, 3072, 4096], P('span', 'cp'), may hold values from -6 to 6
- cache_keys: bfloat16 [3072, 4096], P('span', 'cp'), may hold values from -10 to 10
- cache_values: bfloat16 [3072, 4096], P('span', 'cp'), may hold values from -6 to 6
- gate_table: float32 [64, 4096], replicated, may hold values from -8 to 8
- noise_steps: int32 [4], replicated, may hold values from 0 to 63
- span_order: int32 [4], replicated, may hold values from 0 to 3, each once
- block_mask: int32 [4, 8], replicated, may hold values 0 or 1
Outputs:
- gated_attention: bfloat16 [4, 3072, 4096], P('span', 'cp')
The draws below stay inside these ranges and needn't reach their ends.
Inputs may be any that keep to these rules, and one draw needn't show every extreme that they name: `span_order`: each of 0 to 3 once.
All inputs are finite; a program needn't handle non-finite values.
Results may differ from the reference program's by a relative error of at most 0.0055.
Values may be sent and summed in bfloat16 or wider, within the bound.
No kernel may reach another device: no remote copies, remote signals or barrier semaphores. Data moves between devices by JAX's collectives and lax.ppermute only.
A program may use at most 128 MiB of HBM per device.

```python
import math
import jax
import jax.numpy as jnp
from jax import lax

H = 32
HD = 128
NBLK = 8
STEPS = 64
SPANS = 4
SPAN_TOK = 3072
BLK_TOK = 384


def draw_queries(key, part):
    key = jax.random.fold_in(key, 1)
    first_key = jax.random.fold_in(key, 0)
    shape = (SPANS, SPAN_TOK, H * HD)
    base = jnp.clip(1.6 * jax.random.normal(first_key, shape, jnp.float32), -10.0, 10.0)
    return base.astype(jnp.bfloat16)


def draw_keys(key, part):
    key = jax.random.fold_in(key, 2)
    first_key = jax.random.fold_in(key, 0)
    shape = (SPANS, SPAN_TOK, H * HD)
    base = jnp.clip(1.6 * jax.random.normal(first_key, shape, jnp.float32), -10.0, 10.0)
    return base.astype(jnp.bfloat16)


def touch_ends(values, key, low, largest):
    longest = values.shape.index(max(values.shape))
    spots = []
    for shift in (0, 1):
        where = [jax.random.randint(jax.random.fold_in(key, axis), (), 0, length) for axis, length in enumerate(values.shape)]
        where[longest] = (where[longest] + shift) % values.shape[longest]
        spots.append(tuple(where))
    return values.at[spots[0]].set(low).at[spots[1]].set(largest)


def block_scale(rng, shape, cuts, smallest, high):
    def one(axis_at, shards_of):
        steps = jax.random.uniform(jax.random.fold_in(jax.random.fold_in(rng, 6), axis_at), (shards_of,), jnp.float32, smallest / len(cuts), high / len(cuts))
        return jnp.repeat(jnp.exp(steps), shape[axis_at] // shards_of).reshape((-1,) + (1,) * (len(shape) - axis_at - 1))

    loudness = one(*cuts[0])
    for cut in cuts[1:]:
        loudness = loudness * one(*cut)
    return loudness


def centred(rng, extent, width, most, shards=(), kind=jnp.bfloat16):
    entries = width * jax.random.normal(rng, extent, jnp.float32)
    if shards:
        entries = entries * block_scale(rng, extent, shards, -0.22, 0.18)
    return jnp.clip(entries, -most, most).astype(kind)


def setup_inputs(seed: int = 0) -> dict:
    arg_keys = jax.random.split(jax.random.key(seed), 10)
    return {
        "queries": draw_queries(jax.random.fold_in(arg_keys[9], 71), 0),
        "keys": draw_keys(jax.random.fold_in(arg_keys[9], 71), 0),
        "values": centred(arg_keys[2], (SPANS, SPAN_TOK, H * HD), 1.0, 6.0, ((0, 4), (1, 32))),
        "cache_keys": centred(arg_keys[3], (SPAN_TOK, H * HD), 1.6, 10.0, ((0, 4), (1, 32))),
        "cache_values": centred(arg_keys[4], (SPAN_TOK, H * HD), 1.0, 6.0, ((0, 4), (1, 32))),
        "gate_table": centred(arg_keys[5], (STEPS, H * HD), 2.0, 8.0, (), jnp.float32),
        "noise_steps": touch_ends(jax.random.randint(arg_keys[6], (SPANS,), 0, STEPS), jax.random.fold_in(arg_keys[6], 1), 0, STEPS - 1).astype(jnp.int32),
        "span_order": jax.random.permutation(arg_keys[7], SPANS).astype(jnp.int32),
        "block_mask": touch_ends((jax.random.randint(arg_keys[8], (SPANS, NBLK), 0, 4) < 3).astype(jnp.int32), jax.random.fold_in(arg_keys[8], 1), 0, 1),
    }


def reference(queries, keys, values, cache_keys, cache_values, gate_table, noise_steps, span_order, block_mask):
    span_tokens = queries.shape[1]
    score_scale = 1.0 / math.sqrt(HD)
    all_keys = jnp.concatenate([keys.reshape(SPANS * span_tokens, H, HD), cache_keys.reshape(span_tokens, H, HD)], 0)
    all_values = jnp.concatenate([values.reshape(SPANS * span_tokens, H, HD), cache_values.reshape(span_tokens, H, HD)], 0)
    key_span = jnp.arange(SPANS * span_tokens, dtype=jnp.int32) // span_tokens
    cache_block = jnp.arange(span_tokens, dtype=jnp.int32) // BLK_TOK
    results = []
    for member in range(SPANS):
        visible = jnp.concatenate([span_order[key_span] <= span_order[member], block_mask[member][cache_block] == 1])
        query_rows = queries[member].reshape(span_tokens, H, HD)

        def per_head(head_index):
            query_head = lax.dynamic_index_in_dim(query_rows, head_index, 1, keepdims=False)
            key_head = lax.dynamic_index_in_dim(all_keys, head_index, 1, keepdims=False)
            value_head = lax.dynamic_index_in_dim(all_values, head_index, 1, keepdims=False)
            scores = jnp.dot(query_head, key_head.T, preferred_element_type=jnp.float32) * score_scale
            scores = jnp.where(visible[None, :], scores, -1e+30)
            weights = jnp.exp(scores - lax.optimization_barrier(jnp.max(scores, axis=1, keepdims=True)))
            totals = lax.optimization_barrier(jnp.sum(weights, axis=1, keepdims=True))
            summed = jnp.dot(weights.astype(jnp.bfloat16), value_head, preferred_element_type=jnp.float32)
            return (summed / totals).astype(jnp.bfloat16)
        attention = lax.map(per_head, jnp.arange(H, dtype=jnp.int32))
        attention = jnp.transpose(attention, (1, 0, 2)).reshape(span_tokens, H * HD)
        gate_row = gate_table[noise_steps[member]]
        results.append((attention.astype(jnp.float32) * gate_row[None, :]).astype(jnp.bfloat16))
    return jnp.stack(results)
```

```python
import math

import jax
import jax.numpy as jnp
from jax import lax
from jax.experimental import pallas as pl
from jax.experimental.pallas import tpu as pltpu
from jax.sharding import PartitionSpec as P

H = 32
HD = 128
NBLK = 8
SPANS = 4
ROWS = 768
HALF = 1536
SPAN_TOK = 3072
BLK = SPAN_TOK // NBLK
SUB = 256
SCALE = math.log2(math.e) / math.sqrt(HD)
LOW = -1e30
NT = (((1,), (1,)), ((), ()))
CORE_SWAP = [(0, 1), (1, 0), (2, 3), (3, 2)]
CHIP_SWAP = [(0, 2), (2, 0), (1, 3), (3, 1)]


def lane_sums(p):
    total = p[:, :HD]
    for t in range(1, p.shape[1] // HD):
        total = total + p[:, t * HD : (t + 1) * HD]
    return total


def attention_kernel(
    order, by_order, seen, q_ref, ka, va, kb, vb, ck, cv, o_ref, q2_s, m_s, l_s, acc_s
):
    c = pl.program_id(0)
    x = q_ref[...].astype(jnp.float32) * SCALE
    hi = x.astype(jnp.bfloat16)
    lo = (x - hi.astype(jnp.float32)).astype(jnp.bfloat16)
    q2_s[...] = jnp.concatenate([hi, lo], axis=1)
    count = order[c] + 1
    parts = [slice(j * SUB, (j + 1) * SUB) for j in range(ROWS // SUB)]

    def scores(rows, k):
        k2 = jnp.concatenate([k, k], axis=1)
        return lax.dot_general(q2_s[rows, :], k2, NT, preferred_element_type=jnp.float32)

    def half(ref, span):
        return ref[span].reshape(HALF, HD)

    def both(ref_a, ref_b, span):
        return jnp.concatenate([half(ref_a, span), half(ref_b, span)], axis=0)

    first = half(ka, c)[:SUB]
    for rows in parts:
        top = jnp.max(scores(rows, first), axis=1, keepdims=True)
        m_s[rows, :] = jnp.broadcast_to(top, (SUB, HD))
    l_s[...] = jnp.zeros_like(l_s)
    acc_s[...] = jnp.zeros_like(acc_s)

    def add(rows, p, v):
        l_s[rows, :] += lane_sums(p)
        acc_s[rows, :] += jnp.dot(p.astype(jnp.bfloat16), v, preferred_element_type=jnp.float32)

    def span_step(i, carry):
        span = by_order[i]
        k = both(ka, kb, span)
        v = both(va, vb, span)
        for rows in parts:
            shift = jnp.concatenate([m_s[rows, :]] * (SPAN_TOK // HD), axis=1)
            add(rows, jnp.exp2(scores(rows, k) - shift), v)
        return carry

    lax.fori_loop(0, count, span_step, 0)
    any_seen = seen[c, 0]
    for b in range(1, NBLK):
        any_seen = any_seen + seen[c, b]

    @pl.when(any_seen > 0)
    def _():
        k = ck[...]
        v = cv[...]
        for rows in parts:
            m = m_s[rows, :]
            shift = []
            for b in range(NBLK):
                shift += [jnp.where(seen[c, b] > 0, m, -LOW)] * (BLK // HD)
            add(rows, jnp.exp2(scores(rows, k) - jnp.concatenate(shift, axis=1)), v)

    fits = jnp.sum(l_s[...], axis=1, keepdims=True) < 2.0**100
    bad = jnp.max(jnp.where(fits, 0.0, 1.0))

    @pl.when(bad > 0.0)
    def _():
        m_s[...] = jnp.full_like(m_s, LOW)
        l_s[...] = jnp.zeros_like(l_s)
        acc_s[...] = jnp.zeros_like(acc_s)

        def careful(k, v):
            for rows in parts:
                s = scores(rows, k)
                m = m_s[rows, :]
                top = jnp.maximum(m, jnp.max(s, axis=1, keepdims=True))
                rescale = jnp.exp2(m - top)
                m_s[rows, :] = top
                l_s[rows, :] *= rescale
                acc_s[rows, :] *= rescale
                add(rows, jnp.exp2(s - jnp.concatenate([top] * (k.shape[0] // HD), axis=1)), v)

        def careful_span(i, carry):
            span = by_order[i]
            careful(half(ka, span), half(va, span))
            careful(half(kb, span), half(vb, span))
            return carry

        lax.fori_loop(0, count, careful_span, 0)

        def careful_block(b, carry):
            @pl.when(seen[c, b] > 0)
            def _():
                rows = pl.ds(pl.multiple_of(b * BLK, BLK), BLK)
                careful(ck[rows, :], cv[rows, :])

            return carry

        lax.fori_loop(0, NBLK, careful_block, 0)

    total = jnp.sum(l_s[...], axis=1, keepdims=True)
    o_ref[...] = (acc_s[...] / total).astype(o_ref.dtype)


def attention(order, by_order, seen, q, mine, other, ck, cv):
    whole = lambda part: pl.BlockSpec((SPANS, H, 1, 48, HD), lambda c, *_: (0, 0, part, 0, 0))
    cached = pl.BlockSpec((SPAN_TOK, HD), lambda c, *_: (0, 0))
    rows = pl.BlockSpec((ROWS, HD), lambda c, *_: (c, 0))
    mine = mine.reshape(SPANS, H, 2, 48, HD)
    other = other.reshape(SPANS, H, 2, 48, HD)
    return pl.pallas_call(
        attention_kernel,
        grid_spec=pltpu.PrefetchScalarGridSpec(
            num_scalar_prefetch=3,
            grid=(SPANS,),
            in_specs=[rows, whole(0), whole(1), whole(0), whole(1), cached, cached],
            out_specs=rows,
            scratch_shapes=[
                pltpu.VMEM((ROWS, 2 * HD), jnp.bfloat16),
                pltpu.VMEM((ROWS, HD), jnp.float32),
                pltpu.VMEM((ROWS, HD), jnp.float32),
                pltpu.VMEM((ROWS, HD), jnp.float32),
            ],
        ),
        out_shape=jax.ShapeDtypeStruct((SPANS * ROWS, HD), jnp.bfloat16),
        compiler_params=pltpu.CompilerParams(vmem_limit_bytes=48 * 2**20),
        cost_estimate=pl.CostEstimate(
            flops=16_000_000_000, bytes_accessed=12_000_000, transcendentals=30_000_000
        ),
        name="attention",
    )(order, by_order, seen, q, mine, mine, other, other, ck, cv)


def on_device(
    queries, keys, values, cache_keys, cache_values, gate_table, noise_steps, span_order, block_mask
):
    everyone = ("span", "cp")
    group = lax.axis_index("span")
    cache = jnp.concatenate([cache_keys, cache_values], axis=0)
    cache = jnp.stack([cache, lax.ppermute(cache, "span", CHIP_SWAP)])
    cache = jnp.concatenate([cache, lax.ppermute(cache, "span", CORE_SWAP)])
    ck = cache[:, :768].reshape(SPAN_TOK, HD)
    cv = cache[:, 768:].reshape(SPAN_TOK, HD)
    holders = jnp.stack([group, group ^ 2, group ^ 1, group ^ 3])
    slots = (holders[:, None] * 2 + jnp.arange(2)[None, :]).reshape(NBLK)
    seen = jnp.take(block_mask, slots, axis=1)
    by_order = jnp.sum(
        jnp.where(span_order[None, :] == jnp.arange(SPANS)[:, None], jnp.arange(SPANS)[None, :], 0),
        axis=1,
    ).astype(jnp.int32)

    q = queries.reshape(SPANS, 24, H, HD).transpose(0, 2, 1, 3).reshape(128, 24, HD)
    k = keys.reshape(2, 48, H, HD).transpose(0, 2, 1, 3)
    v = values.reshape(2, 48, H, HD).transpose(0, 2, 1, 3)
    kv = jnp.concatenate([k, v], axis=2)
    kv = jnp.concatenate([kv, kv], axis=0).reshape(128, 96, HD)
    q = lax.all_to_all(q, everyone, 0, 0, tiled=True)
    kv = lax.all_to_all(kv, everyone, 0, 0, tiled=True)
    other = lax.ppermute(kv, "span", CORE_SWAP)
    out = attention(
        span_order, by_order, seen, q.reshape(SPANS * ROWS, HD), kv, other, ck, cv
    )
    out = lax.all_to_all(out.reshape(128, 24, HD), everyone, 0, 0, tiled=True)
    out = out.reshape(SPANS, H, 24, HD).transpose(0, 2, 1, 3).reshape(96, H * HD)
    step = lax.dynamic_index_in_dim(noise_steps, group, 0, keepdims=False)
    gate_row = lax.dynamic_index_in_dim(gate_table, step, 0, keepdims=True)
    return (out.astype(jnp.float32) * gate_row).astype(jnp.bfloat16)[None]


def solution(mesh):
    placed = (
        P("span", "cp", None),
        P("span", "cp", None),
        P("span", "cp", None),
        P("span", "cp"),
        P("span", "cp"),
        P(),
        P(),
        P(),
        P(),
    )
    return jax.shard_map(
        on_device, mesh=mesh, in_specs=placed, out_specs=P("span", "cp", None), check_vma=False
    )
```

```python
import math

import jax
import jax.numpy as jnp
from jax import lax
from jax.experimental import pallas as pl
from jax.experimental.pallas import tpu as pltpu
from jax.sharding import PartitionSpec as P

H = 32
HD = 128
NBLK = 8
SPANS = 4
ROWS = 768
SPAN_TOK = 3072
BLK = SPAN_TOK // NBLK
PART = 24
SUB = 256
SCALE = math.log2(math.e) / math.sqrt(HD)
LOW = -1e30
NT = (((1,), (1,)), ((), ()))
CORE_SWAP = [(0, 1), (1, 0), (2, 3), (3, 2)]
CHIP_SWAP = [(0, 2), (2, 0), (1, 3), (3, 1)]
EVERYONE = ("span", "cp")
MEMORY = 60 * 2**20


def pack_kernel(k_ref, v_ref, q_ref, o_ref):
    heads = o_ref.shape[1]
    for h in range(heads):
        cols = slice(h * HD, (h + 1) * HD)
        k, v, q = (ref[0, :, cols].astype(jnp.float32) for ref in (k_ref, v_ref, q_ref))
        for s in range(SPANS):
            rows = slice(s * PART, (s + 1) * PART)
            together = jnp.concatenate([k[rows], v[rows], q[rows]], axis=0)
            o_ref[s, h] = together.astype(o_ref.dtype)


def pack(k, v, q):
    step = 16
    return pl.pallas_call(
        pack_kernel,
        grid=(H // step,),
        in_specs=[pl.BlockSpec((1, SPANS * PART, step * HD), lambda j: (0, 0, j))] * 3,
        out_specs=pl.BlockSpec((SPANS, step, 3 * PART, HD), lambda j: (0, j, 0, 0)),
        out_shape=jax.ShapeDtypeStruct((SPANS, H, 3 * PART, HD), jnp.bfloat16),
        compiler_params=pltpu.CompilerParams(vmem_limit_bytes=MEMORY),
        name="pack",
    )(k, v, q)


def gate_kernel(group, steps, x_ref, gate_ref, o_ref):
    heads = x_ref.shape[1]
    row = gate_ref[pl.ds(lax.rem(steps[group[0]], 8), 1), :]
    for h in range(heads):
        cols = slice(h * HD, (h + 1) * HD)
        x = [x_ref[s, h].astype(jnp.float32) for s in range(SPANS)]
        o_ref[0, :, cols] = (jnp.concatenate(x, axis=0) * row[:, cols]).astype(o_ref.dtype)


def apply_gate(group, steps, x, gate_table):
    step = 16
    return pl.pallas_call(
        gate_kernel,
        grid_spec=pltpu.PrefetchScalarGridSpec(
            num_scalar_prefetch=2,
            grid=(H // step,),
            in_specs=[
                pl.BlockSpec((SPANS, step, PART, HD), lambda j, *_: (0, j, 0, 0)),
                pl.BlockSpec(
                    (8, step * HD),
                    lambda j, group, steps: (lax.div(steps[group[0]], 8), j),
                ),
            ],
            out_specs=pl.BlockSpec((1, SPANS * PART, step * HD), lambda j, *_: (0, 0, j)),
        ),
        out_shape=jax.ShapeDtypeStruct((1, SPANS * PART, H * HD), jnp.bfloat16),
        compiler_params=pltpu.CompilerParams(vmem_limit_bytes=MEMORY),
        name="gate",
    )(group, steps, x, gate_table)


def lane_sums(p):
    total = p[:, :HD]
    for t in range(1, p.shape[1] // HD):
        total = total + p[:, t * HD : (t + 1) * HD]
    return total


def wide(column, width):
    return jnp.concatenate([column] * (width // HD), axis=1)


class Block:
    def __init__(self, q2, l, acc):
        self.q2, self.l, self.acc = q2, l, acc
        self.parts = [slice(j, j + SUB) for j in range(0, ROWS, SUB)]

    def load(self, q):
        x = q.astype(jnp.float32) * SCALE
        hi = x.astype(jnp.bfloat16)
        lo = (x - hi.astype(jnp.float32)).astype(jnp.bfloat16)
        self.q2[...] = jnp.concatenate([hi, lo], axis=1)

    def scores(self, rows, k):
        k2 = jnp.concatenate([k, k], axis=1)
        return lax.dot_general(self.q2[rows, :], k2, NT, preferred_element_type=jnp.float32)

    def clear(self):
        self.l[...] = jnp.zeros(self.l.shape, jnp.float32)
        self.acc[...] = jnp.zeros(self.acc.shape, jnp.float32)

    def add(self, rows, p, v):
        self.l[rows, :] += lane_sums(p)
        self.acc[rows, :] += jnp.dot(
            p.astype(jnp.bfloat16), v, preferred_element_type=jnp.float32
        )

    def fast(self, k, v, seen=None):
        for rows in self.parts:
            s = self.scores(rows, k)
            if seen is not None:
                s = jnp.concatenate(
                    [
                        s[:, b * BLK : (b + 1) * BLK] + jnp.where(one > 0, 0.0, LOW)
                        for b, one in enumerate(seen)
                    ],
                    axis=1,
                )
            self.add(rows, jnp.exp2(s), v)

    def careful(self, m, k, v):
        for rows in self.parts:
            s = self.scores(rows, k)
            old = m[rows, :]
            top = jnp.maximum(old, jnp.max(s, axis=1, keepdims=True))
            rescale = jnp.exp2(old - top)
            m[rows, :] = top
            self.l[rows, :] *= rescale
            self.acc[rows, :] *= rescale
            self.add(rows, jnp.exp2(s - wide(top, k.shape[0])), v)

    def finish(self, o_ref):
        total = jnp.sum(self.l[...], axis=1, keepdims=True)
        o_ref[...] = (self.acc[...] / total).astype(o_ref.dtype)
        fits = (total < 2.0**100) & (total > 2.0**-100)
        return jnp.max(jnp.where(fits, 0.0, 1.0)) > 0.0


def span_at(order, position):
    found = jnp.int32(0)
    for c in range(1, SPANS):
        found = jnp.where(order[c] == position, c, found)
    return found


class Loads:
    def __init__(self, groups, sems):
        self.groups, self.sems = groups, sems

    def copies(self, g):
        return [
            pltpu.make_async_copy(src, dst, self.sems.at[g, n])
            for n, (src, dst) in enumerate(self.groups(g))
        ]

    def start(self, g):
        for copy in self.copies(g):
            copy.start()

    def wait(self, g):
        for copy in self.copies(g):
            copy.wait()


def span_loads(ka, va, kb, vb, k_s, v_s, sems):
    low, high = pl.ds(0, ROWS), pl.ds(ROWS, ROWS)

    def group(span):
        return [
            (ka.at[span], k_s.at[span, low]),
            (kb.at[span], k_s.at[span, high]),
            (va.at[span], v_s.at[span, low]),
            (vb.at[span], v_s.at[span, high]),
        ]

    return Loads(group, sems)


def blocks_seen(group, mask, c):
    holders = [lax.bitwise_xor(group[0], jnp.int32(x)) for x in (0, 2, 1, 3)]
    return [mask[c, holder * 2 + b] for holder in holders for b in range(2)]


def over_spans(order, c, loads, block, k_s, v_s):
    count = order[c] + 1

    def arrive(i):
        @pl.when(c == 0)
        def _():
            loads.wait(span_at(order, i))

    def two(i, carry):
        arrive(2 * i)
        arrive(2 * i + 1)
        one, other = span_at(order, 2 * i), span_at(order, 2 * i + 1)
        block.fast(
            jnp.concatenate([k_s[one], k_s[other]], axis=0),
            jnp.concatenate([v_s[one], v_s[other]], axis=0),
        )
        return carry

    lax.fori_loop(0, lax.div(count, 2), two, 0)

    @pl.when(lax.rem(count, 2) == 1)
    def _():
        arrive(count - 1)
        span = span_at(order, count - 1)
        block.fast(k_s[span], v_s[span])

    def rest(i, carry):
        arrive(i)
        return carry

    lax.fori_loop(count, SPANS, rest, 0)


def near_kernel(group, order, mask, q, ka, va, kb, vb, here, there, *refs):
    l_out, acc_out, q2, l, acc, q_s, k_s, v_s, ck_s, cv_s, q_sems, sems, cache_sems, out_sems = refs
    queries = Loads(lambda c: [(q.at[c], q_s.at[c])], q_sems)
    loads = span_loads(ka, va, kb, vb, k_s, v_s, sems)

    def cache_parts(x):
        rows = pl.ds(x * ROWS, ROWS)
        held, chip = (here, there)[x // 2], x % 2
        return [(held.at[2 * chip], ck_s.at[rows]), (held.at[2 * chip + 1], cv_s.at[rows])]

    cache = Loads(cache_parts, cache_sems)
    results = Loads(lambda c: [(l.at[c], l_out.at[c]), (acc.at[c], acc_out.at[c])], out_sems)
    queries.start(0)
    for x in range(SPANS):
        cache.start(x)
    queries.wait(0)
    for x in range(SPANS):
        cache.wait(x)
    for i in range(SPANS):
        loads.start(span_at(order, i))
    for c in range(1, SPANS):
        queries.start(c)

    def one_span(c, carry):
        @pl.when(c > 0)
        def _():
            queries.wait(c)

        block = Block(q2, l.at[c], acc.at[c])
        block.load(q_s[c])
        block.clear()
        seen = blocks_seen(group, mask, c)

        @pl.when(sum(seen) > 0)
        def _():
            block.fast(ck_s[...], cv_s[...], seen)

        over_spans(order, c, loads, block, k_s, v_s)
        results.start(c)
        return carry

    lax.fori_loop(0, SPANS, one_span, 0)
    for c in range(SPANS):
        results.wait(c)


def far_kernel(group, order, mask, q, *refs):
    spans = refs[:8]
    ka, va, kb, vb = spans[4:]
    here, there, l_in, acc_in, o_ref, q2, l, acc, q_s, k_s, v_s = refs[8:19]
    q_sems, sems, in_sems, m, k_x, v_x, x_sems = refs[19:]
    loads = span_loads(ka, va, kb, vb, k_s, v_s, sems)
    state = Loads(
        lambda c: [(q.at[c], q_s.at[c]), (l_in.at[c], l.at[c]), (acc_in.at[c], acc.at[c])], in_sems
    )
    state.start(0)
    loads.start(span_at(order, 0))
    state.wait(0)
    for i in range(1, SPANS):
        loads.start(span_at(order, i))
    for c in range(1, SPANS):
        state.start(c)

    def one_span(c, carry):
        count = order[c] + 1

        @pl.when(c > 0)
        def _():
            state.wait(c)

        block = Block(q2, l.at[c], acc.at[c])
        block.load(q_s[c])
        over_spans(order, c, loads, block, k_s, v_s)

        @pl.when(block.finish(o_ref.at[c]))
        def _():
            block.clear()
            m[...] = jnp.full(m.shape, LOW, jnp.float32)

            def fetch(k, v):
                piece = Loads(lambda _: [(k, k_x), (v, v_x)], x_sems)
                piece.start(0)
                piece.wait(0)

            def careful_step(i, carry):
                span = span_at(order, i)
                for quarter in range(4):
                    fetch(spans[2 * quarter].at[span], spans[2 * quarter + 1].at[span])
                    block.careful(m, k_x[...], v_x[...])
                return carry

            lax.fori_loop(0, count, careful_step, 0)
            seen = blocks_seen(group, mask, c)
            for x in range(SPANS):
                held, chip = (here, there)[x // 2], x % 2
                fetch(held.at[2 * chip], held.at[2 * chip + 1])
                for b in range(2):

                    @pl.when(seen[2 * x + b] > 0)
                    def _():
                        rows = slice(b * BLK, (b + 1) * BLK)
                        block.careful(m, k_x[rows, :], v_x[rows, :])

            block.finish(o_ref.at[c])

        return carry

    lax.fori_loop(0, SPANS, one_span, 0)


def call(kernel, name, scalars, arrays, outs, out_space, scratch, flops):
    return pl.pallas_call(
        kernel,
        grid_spec=pltpu.PrefetchScalarGridSpec(
            num_scalar_prefetch=len(scalars),
            grid=(),
            in_specs=[pl.BlockSpec(memory_space=pl.ANY)] * len(arrays),
            out_specs=[pl.BlockSpec(memory_space=out_space)] * len(outs),
            scratch_shapes=[pltpu.VMEM((ROWS, 2 * HD), jnp.bfloat16)] + scratch,
        ),
        out_shape=[jax.ShapeDtypeStruct((SPANS, ROWS, HD), dtype) for dtype in outs],
        compiler_params=pltpu.CompilerParams(vmem_limit_bytes=MEMORY),
        cost_estimate=pl.CostEstimate(
            flops=flops, bytes_accessed=12_000_000, transcendentals=20_000_000
        ),
        name=name,
    )(*scalars, *arrays)


def sems(*shape):
    return pltpu.SemaphoreType.DMA(shape)


STATE = [pltpu.VMEM((SPANS, ROWS, HD), jnp.float32)] * 2
QUERIES = [pltpu.VMEM((SPANS, ROWS, HD), jnp.bfloat16)]
SPAN_KEYS = [pltpu.VMEM((SPANS, 2 * ROWS, HD), jnp.bfloat16)] * 2
CACHE_KEYS = [pltpu.VMEM((SPAN_TOK, HD), jnp.bfloat16)] * 2
CAREFUL = [pltpu.VMEM((ROWS, HD), jnp.float32)] + [pltpu.VMEM((ROWS, HD), jnp.bfloat16)] * 2


def near(group, order, mask, q, spans, cached):
    return call(
        near_kernel, "near", [group, order, mask], [q, *spans, *cached],
        [jnp.float32] * 2, pl.ANY,
        STATE + QUERIES + SPAN_KEYS + CACHE_KEYS
        + [sems(SPANS, 1), sems(SPANS, 4), sems(SPANS, 2), sems(SPANS, 2)],
        29_000_000_000,
    )


def far(group, order, mask, q, spans, cached, state):
    return call(
        far_kernel, "far", [group, order, mask], [q, *spans, *cached, *state],
        [jnp.bfloat16], pltpu.VMEM,
        STATE + QUERIES + SPAN_KEYS + [sems(SPANS, 1), sems(SPANS, 4), sems(SPANS, 3)]
        + CAREFUL + [sems(1, 2)],
        17_000_000_000,
    )[0]


def on_device(
    queries, keys, values, cache_keys, cache_values, gate_table, noise_steps, span_order, block_mask
):
    group = jnp.reshape(lax.axis_index("span"), (1,)).astype(jnp.int32)
    apart = [lax.ppermute(x, "span", CHIP_SWAP) for x in (cache_keys, cache_values)]
    sent = pack(keys, values, queries).reshape(SPANS * H, 3 * PART, HD)
    sent, apart = lax.optimization_barrier((sent, apart))
    got = lax.all_to_all(sent, EVERYONE, 0, 0, tiled=True)
    cached = jnp.stack([cache_keys, cache_values, *apart])
    cached = [cached, lax.ppermute(cached, "span", CORE_SWAP)]
    k0, v0, q = (got[:, i * PART : (i + 1) * PART].reshape(SPANS, ROWS, HD) for i in range(3))
    k1, v1 = (lax.ppermute(x, "span", CORE_SWAP) for x in (k0, v0))
    k2, v2 = (lax.ppermute(x, "span", CHIP_SWAP) for x in (k0, v0))

    state = near(group, span_order, block_mask, q, [k0, v0, k1, v1], cached)
    k2, v2, state = lax.optimization_barrier((k2, v2, state))
    k3, v3 = (lax.ppermute(x, "span", CORE_SWAP) for x in (k2, v2))
    out = far(
        group, span_order, block_mask, q, [k0, v0, k1, v1, k2, v2, k3, v3], cached, state
    )
    out = lax.all_to_all(out.reshape(SPANS * H, PART, HD), EVERYONE, 0, 0, tiled=True)
    return apply_gate(group, noise_steps, out.reshape(SPANS, H, PART, HD), gate_table)


def solution(mesh):
    placed = (
        P("span", "cp", None),
        P("span", "cp", None),
        P("span", "cp", None),
        P("span", "cp"),
        P("span", "cp"),
        P(),
        P(),
        P(),
        P(),
    )
    return jax.shard_map(
        on_device, mesh=mesh, in_specs=placed, out_specs=P("span", "cp", None), check_vma=False
    )
```

```python
import math

import jax
import jax.numpy as jnp
from jax import lax
from jax.experimental import pallas as pl
from jax.experimental.pallas import tpu as pltpu
from jax.sharding import PartitionSpec as P

H = 32
HD = 128
NBLK = 8
SPANS = 4
ROWS = 768
SPAN_TOK = 3072
BLK = SPAN_TOK // NBLK
PART = 24
SUB = 256
SCALE = math.log2(math.e) / math.sqrt(HD)
LOW = -1e30
NT = (((1,), (1,)), ((), ()))
CORE_SWAP = [(0, 1), (1, 0), (2, 3), (3, 2)]
CHIP_SWAP = [(0, 2), (2, 0), (1, 3), (3, 1)]
EVERYONE = ("span", "cp")
MEMORY = 60 * 2**20


def pack_kernel(k_ref, v_ref, q_ref, o_ref):
    heads = o_ref.shape[1]
    for h in range(heads):
        cols = slice(h * HD, (h + 1) * HD)
        k, v, q = (ref[0, :, cols].astype(jnp.float32) for ref in (k_ref, v_ref, q_ref))
        for s in range(SPANS):
            rows = slice(s * PART, (s + 1) * PART)
            together = jnp.concatenate([k[rows], v[rows], q[rows]], axis=0)
            o_ref[s, h] = together.astype(o_ref.dtype)


def pack(k, v, q):
    step = 16
    return pl.pallas_call(
        pack_kernel,
        grid=(H // step,),
        in_specs=[pl.BlockSpec((1, SPANS * PART, step * HD), lambda j: (0, 0, j))] * 3,
        out_specs=pl.BlockSpec((SPANS, step, 3 * PART, HD), lambda j: (0, j, 0, 0)),
        out_shape=jax.ShapeDtypeStruct((SPANS, H, 3 * PART, HD), jnp.bfloat16),
        compiler_params=pltpu.CompilerParams(vmem_limit_bytes=MEMORY),
        name="pack",
    )(k, v, q)


def gate_kernel(group, steps, x_ref, gate_ref, o_ref):
    heads = x_ref.shape[1]
    row = gate_ref[pl.ds(lax.rem(steps[group[0]], 8), 1), :]
    for h in range(heads):
        cols = slice(h * HD, (h + 1) * HD)
        x = [x_ref[s, h].astype(jnp.float32) for s in range(SPANS)]
        o_ref[0, :, cols] = (jnp.concatenate(x, axis=0) * row[:, cols]).astype(o_ref.dtype)


def apply_gate(group, steps, x, gate_table):
    step = 16
    return pl.pallas_call(
        gate_kernel,
        grid_spec=pltpu.PrefetchScalarGridSpec(
            num_scalar_prefetch=2,
            grid=(H // step,),
            in_specs=[
                pl.BlockSpec((SPANS, step, PART, HD), lambda j, *_: (0, j, 0, 0)),
                pl.BlockSpec(
                    (8, step * HD),
                    lambda j, group, steps: (lax.div(steps[group[0]], 8), j),
                ),
            ],
            out_specs=pl.BlockSpec((1, SPANS * PART, step * HD), lambda j, *_: (0, 0, j)),
        ),
        out_shape=jax.ShapeDtypeStruct((1, SPANS * PART, H * HD), jnp.bfloat16),
        compiler_params=pltpu.CompilerParams(vmem_limit_bytes=MEMORY),
        name="gate",
    )(group, steps, x, gate_table)


def lane_sums(p):
    total = p[:, :HD]
    for t in range(1, p.shape[1] // HD):
        total = total + p[:, t * HD : (t + 1) * HD]
    return total


def wide(column, width):
    return jnp.concatenate([column] * (width // HD), axis=1)


class Block:
    def __init__(self, q2, l, acc):
        self.q2, self.l, self.acc = q2, l, acc
        self.parts = [slice(j, j + SUB) for j in range(0, ROWS, SUB)]

    def load(self, q):
        x = q.astype(jnp.float32) * SCALE
        hi = x.astype(jnp.bfloat16)
        lo = (x - hi.astype(jnp.float32)).astype(jnp.bfloat16)
        self.q2[...] = jnp.concatenate([hi, lo], axis=1)

    def scores(self, rows, k):
        k2 = jnp.concatenate([k, k], axis=1)
        return lax.dot_general(self.q2[rows, :], k2, NT, preferred_element_type=jnp.float32)

    def clear(self):
        self.l[...] = jnp.zeros(self.l.shape, jnp.float32)
        self.acc[...] = jnp.zeros(self.acc.shape, jnp.float32)

    def add(self, rows, p, v):
        self.l[rows, :] += lane_sums(p)
        self.acc[rows, :] += jnp.dot(
            p.astype(jnp.bfloat16), v, preferred_element_type=jnp.float32
        )

    def fast(self, k, v, seen=None):
        for rows in self.parts:
            s = self.scores(rows, k)
            if seen is not None:
                s = jnp.concatenate(
                    [
                        s[:, b * BLK : (b + 1) * BLK] + jnp.where(one > 0, 0.0, LOW)
                        for b, one in enumerate(seen)
                    ],
                    axis=1,
                )
            self.add(rows, jnp.exp2(s), v)

    def careful(self, m, k, v):
        for rows in self.parts:
            s = self.scores(rows, k)
            old = m[rows, :]
            top = jnp.maximum(old, jnp.max(s, axis=1, keepdims=True))
            rescale = jnp.exp2(old - top)
            m[rows, :] = top
            self.l[rows, :] *= rescale
            self.acc[rows, :] *= rescale
            self.add(rows, jnp.exp2(s - wide(top, k.shape[0])), v)

    def finish(self, o_ref):
        total = jnp.sum(self.l[...], axis=1, keepdims=True)
        o_ref[...] = (self.acc[...] / total).astype(o_ref.dtype)
        fits = (total < 2.0**100) & (total > 2.0**-100)
        return jnp.max(jnp.where(fits, 0.0, 1.0)) > 0.0


def span_at(order, position):
    found = jnp.int32(0)
    for c in range(1, SPANS):
        found = jnp.where(order[c] == position, c, found)
    return found


class Loads:
    def __init__(self, groups, sems):
        self.groups, self.sems = groups, sems

    def copies(self, g):
        return [
            pltpu.make_async_copy(src, dst, self.sems.at[g, n])
            for n, (src, dst) in enumerate(self.groups(g))
        ]

    def start(self, g):
        for copy in self.copies(g):
            copy.start()

    def wait(self, g):
        for copy in self.copies(g):
            copy.wait()


def span_loads(kv_a, kv_b, k_s, v_s, sems):
    low, high = pl.ds(0, ROWS), pl.ds(ROWS, ROWS)

    def group(span):
        return [
            (kv_a.at[0, span], k_s.at[span, low]),
            (kv_b.at[0, span], k_s.at[span, high]),
            (kv_a.at[1, span], v_s.at[span, low]),
            (kv_b.at[1, span], v_s.at[span, high]),
        ]

    return Loads(group, sems)


def blocks_seen(group, mask, c):
    holders = [lax.bitwise_xor(group[0], jnp.int32(x)) for x in (0, 2, 1, 3)]
    return [mask[c, holder * 2 + b] for holder in holders for b in range(2)]


def over_spans(order, c, loads, block, k_s, v_s):
    count = order[c] + 1

    def arrive(i):
        @pl.when(c == 0)
        def _():
            loads.wait(span_at(order, i))

    def two(i, carry):
        arrive(2 * i)
        arrive(2 * i + 1)
        one, other = span_at(order, 2 * i), span_at(order, 2 * i + 1)
        block.fast(
            jnp.concatenate([k_s[one], k_s[other]], axis=0),
            jnp.concatenate([v_s[one], v_s[other]], axis=0),
        )
        return carry

    lax.fori_loop(0, lax.div(count, 2), two, 0)

    @pl.when(lax.rem(count, 2) == 1)
    def _():
        arrive(count - 1)
        span = span_at(order, count - 1)
        block.fast(k_s[span], v_s[span])

    def rest(i, carry):
        arrive(i)
        return carry

    lax.fori_loop(count, SPANS, rest, 0)


def near_kernel(group, order, mask, q, kv_a, kv_b, here, there, *refs):
    l_out, acc_out, q2, l, acc, q_s, k_s, v_s, ck_s, cv_s, q_sems, sems, cache_sems, out_sems = refs
    queries = Loads(lambda c: [(q.at[c], q_s.at[c])], q_sems)
    loads = span_loads(kv_a, kv_b, k_s, v_s, sems)

    def cache_parts(x):
        rows = pl.ds(x * ROWS, ROWS)
        held, chip = (here, there)[x // 2], x % 2
        return [(held.at[2 * chip], ck_s.at[rows]), (held.at[2 * chip + 1], cv_s.at[rows])]

    cache = Loads(cache_parts, cache_sems)
    results = Loads(lambda c: [(l.at[c], l_out.at[c]), (acc.at[c], acc_out.at[c])], out_sems)
    queries.start(0)
    for x in range(SPANS):
        cache.start(x)
    queries.wait(0)
    for x in range(SPANS):
        cache.wait(x)
    for i in range(SPANS):
        loads.start(span_at(order, i))
    for c in range(1, SPANS):
        queries.start(c)

    def one_span(c, carry):
        @pl.when(c > 0)
        def _():
            queries.wait(c)

        block = Block(q2, l.at[c], acc.at[c])
        block.load(q_s[c])
        block.clear()
        seen = blocks_seen(group, mask, c)

        @pl.when(sum(seen) > 0)
        def _():
            block.fast(ck_s[...], cv_s[...], seen)

        over_spans(order, c, loads, block, k_s, v_s)
        results.start(c)
        return carry

    lax.fori_loop(0, SPANS, one_span, 0)
    for c in range(SPANS):
        results.wait(c)


def far_kernel(group, order, mask, q, *refs):
    spans = refs[:4]
    here, there, l_in, acc_in, o_ref, q2, l, acc, q_s, k_s, v_s = refs[4:15]
    sems, in_sems, m, k_x, v_x, x_sems = refs[15:]
    loads = span_loads(spans[2], spans[3], k_s, v_s, sems)
    state = Loads(
        lambda c: [(q.at[c], q_s.at[c]), (l_in.at[c], l.at[c]), (acc_in.at[c], acc.at[c])], in_sems
    )
    state.start(0)
    loads.start(span_at(order, 0))
    state.wait(0)
    for i in range(1, SPANS):
        loads.start(span_at(order, i))
    for c in range(1, SPANS):
        state.start(c)

    def one_span(c, carry):
        count = order[c] + 1

        @pl.when(c > 0)
        def _():
            state.wait(c)

        block = Block(q2, l.at[c], acc.at[c])
        block.load(q_s[c])
        over_spans(order, c, loads, block, k_s, v_s)

        @pl.when(block.finish(o_ref.at[c]))
        def _():
            block.clear()
            m[...] = jnp.full(m.shape, LOW, jnp.float32)

            def fetch(k, v):
                piece = Loads(lambda _: [(k, k_x), (v, v_x)], x_sems)
                piece.start(0)
                piece.wait(0)

            def careful_step(i, carry):
                span = span_at(order, i)
                for kv in spans:
                    fetch(kv.at[0, span], kv.at[1, span])
                    block.careful(m, k_x[...], v_x[...])
                return carry

            lax.fori_loop(0, count, careful_step, 0)
            seen = blocks_seen(group, mask, c)
            for x in range(SPANS):
                held, chip = (here, there)[x // 2], x % 2
                fetch(held.at[2 * chip], held.at[2 * chip + 1])
                for b in range(2):

                    @pl.when(seen[2 * x + b] > 0)
                    def _():
                        rows = slice(b * BLK, (b + 1) * BLK)
                        block.careful(m, k_x[rows, :], v_x[rows, :])

            block.finish(o_ref.at[c])

        return carry

    lax.fori_loop(0, SPANS, one_span, 0)


def call(kernel, name, scalars, arrays, outs, out_space, scratch, flops):
    return pl.pallas_call(
        kernel,
        grid_spec=pltpu.PrefetchScalarGridSpec(
            num_scalar_prefetch=len(scalars),
            grid=(),
            in_specs=[pl.BlockSpec(memory_space=pl.ANY)] * len(arrays),
            out_specs=[pl.BlockSpec(memory_space=out_space)] * len(outs),
            scratch_shapes=[pltpu.VMEM((ROWS, 2 * HD), jnp.bfloat16)] + scratch,
        ),
        out_shape=[jax.ShapeDtypeStruct((SPANS, ROWS, HD), dtype) for dtype in outs],
        compiler_params=pltpu.CompilerParams(vmem_limit_bytes=MEMORY),
        cost_estimate=pl.CostEstimate(
            flops=flops, bytes_accessed=12_000_000, transcendentals=20_000_000
        ),
        name=name,
    )(*scalars, *arrays)


def sems(*shape):
    return pltpu.SemaphoreType.DMA(shape)


STATE = [pltpu.VMEM((SPANS, ROWS, HD), jnp.float32)] * 2
QUERIES = [pltpu.VMEM((SPANS, ROWS, HD), jnp.bfloat16)]
SPAN_KEYS = [pltpu.VMEM((SPANS, 2 * ROWS, HD), jnp.bfloat16)] * 2
CACHE_KEYS = [pltpu.VMEM((SPAN_TOK, HD), jnp.bfloat16)] * 2
CAREFUL = [pltpu.VMEM((ROWS, HD), jnp.float32)] + [pltpu.VMEM((ROWS, HD), jnp.bfloat16)] * 2


def near(group, order, mask, q, spans, cached):
    return call(
        near_kernel, "near", [group, order, mask], [q, *spans, *cached],
        [jnp.float32] * 2, pl.ANY,
        STATE + QUERIES + SPAN_KEYS + CACHE_KEYS
        + [sems(SPANS, 1), sems(SPANS, 4), sems(SPANS, 2), sems(SPANS, 2)],
        29_000_000_000,
    )


def far(group, order, mask, q, spans, cached, state):
    return call(
        far_kernel, "far", [group, order, mask], [q, *spans, *cached, *state],
        [jnp.bfloat16], pltpu.VMEM,
        STATE + QUERIES + SPAN_KEYS + [sems(SPANS, 4), sems(SPANS, 3)]
        + CAREFUL + [sems(1, 2)],
        17_000_000_000,
    )[0]


def on_device(
    queries, keys, values, cache_keys, cache_values, gate_table, noise_steps, span_order, block_mask
):
    group = jnp.reshape(lax.axis_index("span"), (1,)).astype(jnp.int32)
    apart = [lax.ppermute(x, "span", CHIP_SWAP) for x in (cache_keys, cache_values)]
    sent = pack(keys, values, queries).reshape(SPANS * H, 3 * PART, HD)
    sent, apart[0] = lax.optimization_barrier((sent, apart[0]))
    got = lax.all_to_all(sent, EVERYONE, 0, 0, tiled=True)
    got, apart = lax.optimization_barrier((got, apart))
    cached = jnp.stack([cache_keys, cache_values, *apart])
    cached = [cached, lax.ppermute(cached, "span", CORE_SWAP)]
    kv0 = got[:, : 2 * PART].reshape(SPANS, H, 2, PART, HD).transpose(2, 0, 1, 3, 4)
    kv0 = kv0.reshape(2, SPANS, ROWS, HD)
    kv2 = lax.ppermute(kv0, "span", CHIP_SWAP)
    kv1 = lax.ppermute(kv0, "span", CORE_SWAP)
    got, kv1 = lax.optimization_barrier((got, kv1))
    q = got[:, 2 * PART :].reshape(SPANS, ROWS, HD)

    state = near(group, span_order, block_mask, q, [kv0, kv1], cached)
    kv2, state = lax.optimization_barrier((kv2, state))
    kv3 = lax.ppermute(kv2, "span", CORE_SWAP)
    out = far(group, span_order, block_mask, q, [kv0, kv1, kv2, kv3], cached, state)
    out = lax.all_to_all(out.reshape(SPANS * H, PART, HD), EVERYONE, 0, 0, tiled=True)
    return apply_gate(group, noise_steps, out.reshape(SPANS, H, PART, HD), gate_table)


def solution(mesh):
    placed = (
        P("span", "cp", None),
        P("span", "cp", None),
        P("span", "cp", None),
        P("span", "cp"),
        P("span", "cp"),
        P(),
        P(),
        P(),
        P(),
    )
    return jax.shard_map(
        on_device, mesh=mesh, in_specs=placed, out_specs=P("span", "cp", None), check_vma=False
    )
```

```python
import math

import jax
import jax.numpy as jnp
from jax import lax
from jax.experimental import pallas as pl
from jax.experimental.pallas import tpu as pltpu
from jax.sharding import PartitionSpec as P

H = 32
HD = 128
NBLK = 8
SPANS = 4
ROWS = 768
SPAN_TOK = 3072
BLK = SPAN_TOK // NBLK
PART = 24
SUB = 256
SCALE = math.log2(math.e) / math.sqrt(HD)
LOW = -1e30
NT = (((1,), (1,)), ((), ()))
CORE_SWAP = [(0, 1), (1, 0), (2, 3), (3, 2)]
CHIP_SWAP = [(0, 2), (2, 0), (1, 3), (3, 1)]
EVERYONE = ("span", "cp")
MEMORY = 60 * 2**20


def pack_kernel(k_ref, v_ref, q_ref, o_ref):
    heads = o_ref.shape[1]
    for h in range(heads):
        cols = slice(h * HD, (h + 1) * HD)
        k, v, q = (ref[0, :, cols].astype(jnp.float32) for ref in (k_ref, v_ref, q_ref))
        for s in range(SPANS):
            rows = slice(s * PART, (s + 1) * PART)
            together = jnp.concatenate([k[rows], v[rows], q[rows]], axis=0)
            o_ref[s, h] = together.astype(o_ref.dtype)


def pack(k, v, q):
    step = 16
    return pl.pallas_call(
        pack_kernel,
        grid=(H // step,),
        in_specs=[pl.BlockSpec((1, SPANS * PART, step * HD), lambda j: (0, 0, j))] * 3,
        out_specs=pl.BlockSpec((SPANS, step, 3 * PART, HD), lambda j: (0, j, 0, 0)),
        out_shape=jax.ShapeDtypeStruct((SPANS, H, 3 * PART, HD), jnp.bfloat16),
        compiler_params=pltpu.CompilerParams(vmem_limit_bytes=MEMORY),
        name="pack",
    )(k, v, q)


def gate_kernel(group, steps, x_ref, gate_ref, o_ref):
    heads = x_ref.shape[1]
    row = gate_ref[pl.ds(lax.rem(steps[group[0]], 8), 1), :]
    for h in range(heads):
        cols = slice(h * HD, (h + 1) * HD)
        x = [x_ref[s, h].astype(jnp.float32) for s in range(SPANS)]
        o_ref[0, :, cols] = (jnp.concatenate(x, axis=0) * row[:, cols]).astype(o_ref.dtype)


def apply_gate(group, steps, x, gate_table):
    step = 16
    return pl.pallas_call(
        gate_kernel,
        grid_spec=pltpu.PrefetchScalarGridSpec(
            num_scalar_prefetch=2,
            grid=(H // step,),
            in_specs=[
                pl.BlockSpec((SPANS, step, PART, HD), lambda j, *_: (0, j, 0, 0)),
                pl.BlockSpec(
                    (8, step * HD),
                    lambda j, group, steps: (lax.div(steps[group[0]], 8), j),
                ),
            ],
            out_specs=pl.BlockSpec((1, SPANS * PART, step * HD), lambda j, *_: (0, 0, j)),
        ),
        out_shape=jax.ShapeDtypeStruct((1, SPANS * PART, H * HD), jnp.bfloat16),
        compiler_params=pltpu.CompilerParams(vmem_limit_bytes=MEMORY),
        name="gate",
    )(group, steps, x, gate_table)


def lane_sums(p):
    total = p[:, :HD]
    for t in range(1, p.shape[1] // HD):
        total = total + p[:, t * HD : (t + 1) * HD]
    return total


def wide(column, width):
    return jnp.concatenate([column] * (width // HD), axis=1)


class Block:
    def __init__(self, q2, l, acc):
        self.q2, self.l, self.acc = q2, l, acc
        self.parts = [slice(j, j + SUB) for j in range(0, ROWS, SUB)]

    def load(self, q):
        x = q.astype(jnp.float32) * SCALE
        hi = x.astype(jnp.bfloat16)
        lo = (x - hi.astype(jnp.float32)).astype(jnp.bfloat16)
        self.q2[...] = jnp.concatenate([hi, lo], axis=1)

    def scores(self, rows, k):
        k2 = jnp.concatenate([k, k], axis=1)
        return lax.dot_general(self.q2[rows, :], k2, NT, preferred_element_type=jnp.float32)

    def clear(self):
        self.l[...] = jnp.zeros(self.l.shape, jnp.float32)
        self.acc[...] = jnp.zeros(self.acc.shape, jnp.float32)

    def add(self, rows, p, v):
        self.l[rows, :] += lane_sums(p)
        self.acc[rows, :] += jnp.dot(
            p.astype(jnp.bfloat16), v, preferred_element_type=jnp.float32
        )

    def fast(self, k, v, seen=None):
        for rows in self.parts:
            s = self.scores(rows, k)
            if seen is not None:
                s = jnp.concatenate(
                    [
                        s[:, b * BLK : (b + 1) * BLK] + jnp.where(one > 0, 0.0, LOW)
                        for b, one in enumerate(seen)
                    ],
                    axis=1,
                )
            self.add(rows, jnp.exp2(s), v)

    def careful(self, m, k, v):
        for rows in self.parts:
            s = self.scores(rows, k)
            old = m[rows, :]
            top = jnp.maximum(old, jnp.max(s, axis=1, keepdims=True))
            rescale = jnp.exp2(old - top)
            m[rows, :] = top
            self.l[rows, :] *= rescale
            self.acc[rows, :] *= rescale
            self.add(rows, jnp.exp2(s - wide(top, k.shape[0])), v)

    def finish(self, o_ref):
        total = jnp.sum(self.l[...], axis=1, keepdims=True)
        o_ref[...] = (self.acc[...] / total).astype(o_ref.dtype)
        fits = (total < 2.0**100) & (total > 2.0**-100)
        return jnp.max(jnp.where(fits, 0.0, 1.0)) > 0.0


def span_at(order, position):
    found = jnp.int32(0)
    for c in range(1, SPANS):
        found = jnp.where(order[c] == position, c, found)
    return found


class Loads:
    def __init__(self, groups, sems):
        self.groups, self.sems = groups, sems

    def copies(self, g):
        return [
            pltpu.make_async_copy(src, dst, self.sems.at[g, n])
            for n, (src, dst) in enumerate(self.groups(g))
        ]

    def start(self, g):
        for copy in self.copies(g):
            copy.start()

    def wait(self, g):
        for copy in self.copies(g):
            copy.wait()


def span_loads(kv_a, kv_b, k_s, v_s, sems):
    low, high = pl.ds(0, ROWS), pl.ds(ROWS, ROWS)

    def group(span):
        return [
            (kv_a.at[0, span], k_s.at[span, low]),
            (kv_b.at[0, span], k_s.at[span, high]),
            (kv_a.at[1, span], v_s.at[span, low]),
            (kv_b.at[1, span], v_s.at[span, high]),
        ]

    return Loads(group, sems)


def blocks_seen(group, mask, c):
    holders = [lax.bitwise_xor(group[0], jnp.int32(x)) for x in (0, 2, 1, 3)]
    return [mask[c, holder * 2 + b] for holder in holders for b in range(2)]


def over_spans(order, c, loads, block, k_s, v_s):
    count = order[c] + 1

    def arrive(i):
        @pl.when(c == 0)
        def _():
            loads.wait(span_at(order, i))

    def two(i, carry):
        arrive(2 * i)
        arrive(2 * i + 1)
        one, other = span_at(order, 2 * i), span_at(order, 2 * i + 1)
        block.fast(
            jnp.concatenate([k_s[one], k_s[other]], axis=0),
            jnp.concatenate([v_s[one], v_s[other]], axis=0),
        )
        return carry

    lax.fori_loop(0, lax.div(count, 2), two, 0)

    @pl.when(lax.rem(count, 2) == 1)
    def _():
        arrive(count - 1)
        span = span_at(order, count - 1)
        block.fast(k_s[span], v_s[span])

    def rest(i, carry):
        arrive(i)
        return carry

    lax.fori_loop(count, SPANS, rest, 0)


def near_kernel(group, order, mask, q, kv_a, kv_b, here, there, *refs):
    l_out, acc_out, q2, l, acc, q_s, k_s, v_s, ck_s, cv_s, q_sems, sems, cache_sems, out_sems = refs
    queries = Loads(lambda c: [(q.at[c], q_s.at[c])], q_sems)
    loads = span_loads(kv_a, kv_b, k_s, v_s, sems)

    def cache_parts(x):
        rows = pl.ds(x * ROWS, ROWS)
        held, chip = (here, there)[x // 2], x % 2
        return [(held.at[2 * chip], ck_s.at[rows]), (held.at[2 * chip + 1], cv_s.at[rows])]

    cache = Loads(cache_parts, cache_sems)
    results = Loads(lambda c: [(l.at[c], l_out.at[c]), (acc.at[c], acc_out.at[c])], out_sems)
    queries.start(0)
    for x in range(SPANS):
        cache.start(x)
    queries.wait(0)
    for x in range(SPANS):
        cache.wait(x)
    for i in range(SPANS):
        loads.start(span_at(order, i))
    for c in range(1, SPANS):
        queries.start(c)

    def one_span(c, carry):
        @pl.when(c > 0)
        def _():
            queries.wait(c)

        block = Block(q2, l.at[c], acc.at[c])
        block.load(q_s[c])
        block.clear()
        seen = blocks_seen(group, mask, c)

        @pl.when(sum(seen) > 0)
        def _():
            block.fast(ck_s[...], cv_s[...], seen)

        over_spans(order, c, loads, block, k_s, v_s)
        results.start(c)
        return carry

    lax.fori_loop(0, SPANS, one_span, 0)
    for c in range(SPANS):
        results.wait(c)


def far_kernel(group, order, mask, q, *refs):
    spans = refs[:4]
    here, there, l_in, acc_in, o_out, q2, l, acc, q_s, k_s, v_s = refs[4:15]
    sems, in_sems, m, k_x, v_x, x_sems, o_s, out_sems = refs[15:]
    results = Loads(lambda c: [(o_s.at[c], o_out.at[c])], out_sems)
    loads = span_loads(spans[2], spans[3], k_s, v_s, sems)
    state = Loads(
        lambda c: [(q.at[c], q_s.at[c]), (l_in.at[c], l.at[c]), (acc_in.at[c], acc.at[c])], in_sems
    )
    loads.start(span_at(order, 0))
    state.start(0)
    state.wait(0)
    for i in range(1, SPANS):
        loads.start(span_at(order, i))
    for c in range(1, SPANS):
        state.start(c)

    def one_span(c, carry):
        count = order[c] + 1

        @pl.when(c > 0)
        def _():
            state.wait(c)

        block = Block(q2, l.at[c], acc.at[c])
        block.load(q_s[c])
        over_spans(order, c, loads, block, k_s, v_s)

        @pl.when(block.finish(o_s.at[c]))
        def _():
            block.clear()
            m[...] = jnp.full(m.shape, LOW, jnp.float32)

            def fetch(k, v):
                piece = Loads(lambda _: [(k, k_x), (v, v_x)], x_sems)
                piece.start(0)
                piece.wait(0)

            def careful_step(i, carry):
                span = span_at(order, i)
                for kv in spans:
                    fetch(kv.at[0, span], kv.at[1, span])
                    block.careful(m, k_x[...], v_x[...])
                return carry

            lax.fori_loop(0, count, careful_step, 0)
            seen = blocks_seen(group, mask, c)
            for x in range(SPANS):
                held, chip = (here, there)[x // 2], x % 2
                fetch(held.at[2 * chip], held.at[2 * chip + 1])
                for b in range(2):

                    @pl.when(seen[2 * x + b] > 0)
                    def _():
                        rows = slice(b * BLK, (b + 1) * BLK)
                        block.careful(m, k_x[rows, :], v_x[rows, :])

            block.finish(o_s.at[c])

        results.start(c)
        return carry

    lax.fori_loop(0, SPANS, one_span, 0)
    for c in range(SPANS):
        results.wait(c)


def call(kernel, name, scalars, arrays, outs, out_space, scratch, flops):
    return pl.pallas_call(
        kernel,
        grid_spec=pltpu.PrefetchScalarGridSpec(
            num_scalar_prefetch=len(scalars),
            grid=(),
            in_specs=[pl.BlockSpec(memory_space=pl.ANY)] * len(arrays),
            out_specs=[pl.BlockSpec(memory_space=out_space)] * len(outs),
            scratch_shapes=[pltpu.VMEM((ROWS, 2 * HD), jnp.bfloat16)] + scratch,
        ),
        out_shape=[jax.ShapeDtypeStruct((SPANS, ROWS, HD), dtype) for dtype in outs],
        compiler_params=pltpu.CompilerParams(vmem_limit_bytes=MEMORY),
        cost_estimate=pl.CostEstimate(
            flops=flops, bytes_accessed=12_000_000, transcendentals=20_000_000
        ),
        name=name,
    )(*scalars, *arrays)


def sems(*shape):
    return pltpu.SemaphoreType.DMA(shape)


STATE = [pltpu.VMEM((SPANS, ROWS, HD), jnp.float32)] * 2
QUERIES = [pltpu.VMEM((SPANS, ROWS, HD), jnp.bfloat16)]
SPAN_KEYS = [pltpu.VMEM((SPANS, 2 * ROWS, HD), jnp.bfloat16)] * 2
CACHE_KEYS = [pltpu.VMEM((SPAN_TOK, HD), jnp.bfloat16)] * 2
CAREFUL = [pltpu.VMEM((ROWS, HD), jnp.float32)] + [pltpu.VMEM((ROWS, HD), jnp.bfloat16)] * 2


def near(group, order, mask, q, spans, cached):
    return call(
        near_kernel, "near", [group, order, mask], [q, *spans, *cached],
        [jnp.float32] * 2, pl.ANY,
        STATE + QUERIES + SPAN_KEYS + CACHE_KEYS
        + [sems(SPANS, 1), sems(SPANS, 4), sems(SPANS, 2), sems(SPANS, 2)],
        29_000_000_000,
    )


def far(group, order, mask, q, spans, cached, state):
    return call(
        far_kernel, "far", [group, order, mask], [q, *spans, *cached, *state],
        [jnp.bfloat16], pl.ANY,
        STATE + QUERIES + SPAN_KEYS + [sems(SPANS, 4), sems(SPANS, 3)]
        + CAREFUL + [sems(1, 2)] + QUERIES + [sems(SPANS, 1)],
        17_000_000_000,
    )[0]


def on_device(
    queries, keys, values, cache_keys, cache_values, gate_table, noise_steps, span_order, block_mask
):
    group = jnp.reshape(lax.axis_index("span"), (1,)).astype(jnp.int32)
    apart = [lax.ppermute(x, "span", CHIP_SWAP) for x in (cache_keys, cache_values)]
    sent = pack(keys, values, queries).reshape(SPANS * H, 3 * PART, HD)
    sent, apart[0] = lax.optimization_barrier((sent, apart[0]))
    got = lax.all_to_all(sent, EVERYONE, 0, 0, tiled=True)
    got, apart = lax.optimization_barrier((got, apart))
    cached = jnp.stack([cache_keys, cache_values, *apart])
    cached = [cached, lax.ppermute(cached, "span", CORE_SWAP)]
    kv0 = got[:, : 2 * PART].reshape(SPANS, H, 2, PART, HD).transpose(2, 0, 1, 3, 4)
    kv0 = kv0.reshape(2, SPANS, ROWS, HD)
    kv2 = lax.ppermute(kv0, "span", CHIP_SWAP)
    kv1 = lax.ppermute(kv0, "span", CORE_SWAP)
    got, kv1 = lax.optimization_barrier((got, kv1))
    q = got[:, 2 * PART :].reshape(SPANS, ROWS, HD)

    state = near(group, span_order, block_mask, q, [kv0, kv1], cached)
    kv2, state = lax.optimization_barrier((kv2, state))
    kv3 = lax.ppermute(kv2, "span", CORE_SWAP)
    out = far(group, span_order, block_mask, q, [kv0, kv1, kv2, kv3], cached, state)
    out = lax.all_to_all(out.reshape(SPANS * H, PART, HD), EVERYONE, 0, 0, tiled=True)
    return apply_gate(group, noise_steps, out.reshape(SPANS, H, PART, HD), gate_table)


def solution(mesh):
    placed = (
        P("span", "cp", None),
        P("span", "cp", None),
        P("span", "cp", None),
        P("span", "cp"),
        P("span", "cp"),
        P(),
        P(),
        P(),
        P(),
    )
    return jax.shard_map(
        on_device, mesh=mesh, in_specs=placed, out_specs=P("span", "cp", None), check_vma=False
    )
```

```python
import math

import jax
import jax.numpy as jnp
from jax import lax
from jax.experimental import pallas as pl
from jax.experimental.pallas import tpu as pltpu
from jax.sharding import PartitionSpec as P

H = 32
HD = 128
NBLK = 8
SPANS = 4
ROWS = 768
SPAN_TOK = 3072
BLK = SPAN_TOK // NBLK
PART = 24
SUB = 256
SCALE = math.log2(math.e) / math.sqrt(HD)
LOW = -1e30
NT = (((1,), (1,)), ((), ()))
CORE_SWAP = [(0, 1), (1, 0), (2, 3), (3, 2)]
CHIP_SWAP = [(0, 2), (2, 0), (1, 3), (3, 1)]
EVERYONE = ("span", "cp")
MEMORY = 60 * 2**20


def pack_kernel(k_ref, v_ref, q_ref, o_ref):
    heads = o_ref.shape[1]
    for h in range(heads):
        cols = slice(h * HD, (h + 1) * HD)
        k, v, q = (ref[0, :, cols].astype(jnp.float32) for ref in (k_ref, v_ref, q_ref))
        for s in range(SPANS):
            rows = slice(s * PART, (s + 1) * PART)
            together = jnp.concatenate([k[rows], v[rows], q[rows]], axis=0)
            o_ref[s, h] = together.astype(o_ref.dtype)


def pack(k, v, q):
    step = 16
    return pl.pallas_call(
        pack_kernel,
        grid=(H // step,),
        in_specs=[pl.BlockSpec((1, SPANS * PART, step * HD), lambda j: (0, 0, j))] * 3,
        out_specs=pl.BlockSpec((SPANS, step, 3 * PART, HD), lambda j: (0, j, 0, 0)),
        out_shape=jax.ShapeDtypeStruct((SPANS, H, 3 * PART, HD), jnp.bfloat16),
        compiler_params=pltpu.CompilerParams(vmem_limit_bytes=MEMORY),
        name="pack",
    )(k, v, q)


def gate_kernel(group, steps, x_ref, gate_ref, o_ref):
    heads = x_ref.shape[1]
    row = gate_ref[pl.ds(lax.rem(steps[group[0]], 8), 1), :]
    for h in range(heads):
        cols = slice(h * HD, (h + 1) * HD)
        x = [x_ref[s, h].astype(jnp.float32) for s in range(SPANS)]
        o_ref[0, :, cols] = (jnp.concatenate(x, axis=0) * row[:, cols]).astype(o_ref.dtype)


def apply_gate(group, steps, x, gate_table):
    step = 16
    return pl.pallas_call(
        gate_kernel,
        grid_spec=pltpu.PrefetchScalarGridSpec(
            num_scalar_prefetch=2,
            grid=(H // step,),
            in_specs=[
                pl.BlockSpec((SPANS, step, PART, HD), lambda j, *_: (0, j, 0, 0)),
                pl.BlockSpec(
                    (8, step * HD),
                    lambda j, group, steps: (lax.div(steps[group[0]], 8), j),
                ),
            ],
            out_specs=pl.BlockSpec((1, SPANS * PART, step * HD), lambda j, *_: (0, 0, j)),
        ),
        out_shape=jax.ShapeDtypeStruct((1, SPANS * PART, H * HD), jnp.bfloat16),
        compiler_params=pltpu.CompilerParams(vmem_limit_bytes=MEMORY),
        name="gate",
    )(group, steps, x, gate_table)


def lane_sums(p):
    total = p[:, :HD]
    for t in range(1, p.shape[1] // HD):
        total = total + p[:, t * HD : (t + 1) * HD]
    return total


def wide(column, width):
    return jnp.concatenate([column] * (width // HD), axis=1)


class Block:
    def __init__(self, q2, l, acc):
        self.q2, self.l, self.acc = q2, l, acc
        self.parts = [slice(j, j + SUB) for j in range(0, ROWS, SUB)]

    def load(self, q):
        x = q.astype(jnp.float32) * SCALE
        hi = x.astype(jnp.bfloat16)
        lo = (x - hi.astype(jnp.float32)).astype(jnp.bfloat16)
        self.q2[...] = jnp.concatenate([hi, lo], axis=1)

    def scores(self, rows, k):
        k2 = jnp.concatenate([k, k], axis=1)
        return lax.dot_general(self.q2[rows, :], k2, NT, preferred_element_type=jnp.float32)

    def clear(self):
        self.l[...] = jnp.zeros(self.l.shape, jnp.float32)
        self.acc[...] = jnp.zeros(self.acc.shape, jnp.float32)

    def add(self, rows, p, v):
        self.l[rows, :] += lane_sums(p)
        self.acc[rows, :] += jnp.dot(
            p.astype(jnp.bfloat16), v, preferred_element_type=jnp.float32
        )

    def fast(self, k, v, seen=None):
        for rows in self.parts:
            s = self.scores(rows, k)
            if seen is not None:
                s = jnp.concatenate(
                    [
                        s[:, b * BLK : (b + 1) * BLK] + jnp.where(one > 0, 0.0, LOW)
                        for b, one in enumerate(seen)
                    ],
                    axis=1,
                )
            self.add(rows, jnp.exp2(s), v)

    def careful(self, m, k, v):
        for rows in self.parts:
            s = self.scores(rows, k)
            old = m[rows, :]
            top = jnp.maximum(old, jnp.max(s, axis=1, keepdims=True))
            rescale = jnp.exp2(old - top)
            m[rows, :] = top
            self.l[rows, :] *= rescale
            self.acc[rows, :] *= rescale
            self.add(rows, jnp.exp2(s - wide(top, k.shape[0])), v)

    def finish(self, o_ref):
        total = jnp.sum(self.l[...], axis=1, keepdims=True)
        o_ref[...] = (self.acc[...] / total).astype(o_ref.dtype)
        fits = (total < 2.0**100) & (total > 2.0**-100)
        return jnp.max(jnp.where(fits, 0.0, 1.0)) > 0.0


def span_at(order, position):
    found = jnp.int32(0)
    for c in range(1, SPANS):
        found = jnp.where(order[c] == position, c, found)
    return found


class Loads:
    def __init__(self, groups, sems):
        self.groups, self.sems = groups, sems

    def copies(self, g):
        return [
            pltpu.make_async_copy(src, dst, self.sems.at[g, n])
            for n, (src, dst) in enumerate(self.groups(g))
        ]

    def start(self, g):
        for copy in self.copies(g):
            copy.start()

    def wait(self, g):
        for copy in self.copies(g):
            copy.wait()


def span_loads(kv_a, kv_b, k_s, v_s, sems):
    low, high = pl.ds(0, ROWS), pl.ds(ROWS, ROWS)

    def group(span):
        return [
            (kv_a.at[0, span], k_s.at[span, low]),
            (kv_b.at[0, span], k_s.at[span, high]),
            (kv_a.at[1, span], v_s.at[span, low]),
            (kv_b.at[1, span], v_s.at[span, high]),
        ]

    return Loads(group, sems)


def blocks_seen(group, mask, c):
    holders = [lax.bitwise_xor(group[0], jnp.int32(x)) for x in (0, 2, 1, 3)]
    return [mask[c, holder * 2 + b] for holder in holders for b in range(2)]


def over_spans(order, c, loads, block, k_s, v_s):
    count = order[c] + 1

    def arrive(i):
        @pl.when(c == 0)
        def _():
            loads.wait(span_at(order, i))

    def two(i, carry):
        arrive(2 * i)
        arrive(2 * i + 1)
        one, other = span_at(order, 2 * i), span_at(order, 2 * i + 1)
        block.fast(
            jnp.concatenate([k_s[one], k_s[other]], axis=0),
            jnp.concatenate([v_s[one], v_s[other]], axis=0),
        )
        return carry

    lax.fori_loop(0, lax.div(count, 2), two, 0)

    @pl.when(lax.rem(count, 2) == 1)
    def _():
        arrive(count - 1)
        span = span_at(order, count - 1)
        block.fast(k_s[span], v_s[span])

    def rest(i, carry):
        arrive(i)
        return carry

    lax.fori_loop(count, SPANS, rest, 0)


def near_kernel(group, order, mask, q, kv_a, kv_b, here, there, *refs):
    l_out, acc_out, q2, l, acc, q_s, k_s, v_s, ck_s, cv_s, q_sems, sems, cache_sems, out_sems = refs
    queries = Loads(lambda c: [(q.at[c], q_s.at[c])], q_sems)
    loads = span_loads(kv_a, kv_b, k_s, v_s, sems)

    def cache_parts(x):
        rows = pl.ds(x * ROWS, ROWS)
        held, chip = (here, there)[x // 2], x % 2
        return [(held.at[2 * chip], ck_s.at[rows]), (held.at[2 * chip + 1], cv_s.at[rows])]

    cache = Loads(cache_parts, cache_sems)
    results = Loads(lambda c: [(l.at[c], l_out.at[c]), (acc.at[c], acc_out.at[c])], out_sems)
    queries.start(0)
    for x in range(SPANS):
        cache.start(x)
    queries.wait(0)
    for x in range(SPANS):
        cache.wait(x)
    for i in range(SPANS):
        loads.start(span_at(order, i))
    for c in range(1, SPANS):
        queries.start(c)

    def one_span(c, carry):
        @pl.when(c > 0)
        def _():
            queries.wait(c)

        block = Block(q2, l.at[c], acc.at[c])
        block.load(q_s[c])
        block.clear()
        seen = blocks_seen(group, mask, c)

        @pl.when(sum(seen) > 0)
        def _():
            block.fast(ck_s[...], cv_s[...], seen)

        over_spans(order, c, loads, block, k_s, v_s)
        results.start(c)
        return carry

    lax.fori_loop(0, SPANS, one_span, 0)
    for c in range(SPANS):
        results.wait(c)


def far_kernel(group, order, mask, q, *refs):
    spans = refs[:4]
    here, there, l_in, acc_in, o_out, q2, l, acc, q_s, k_s, v_s = refs[4:15]
    sems, in_sems, m, k_x, v_x, x_sems, o_s, out_sems = refs[15:]
    results = Loads(lambda c: [(o_s.at[c], o_out.at[c])], out_sems)
    loads = span_loads(spans[2], spans[3], k_s, v_s, sems)
    state = Loads(
        lambda c: [(q.at[c], q_s.at[c]), (l_in.at[c], l.at[c]), (acc_in.at[c], acc.at[c])], in_sems
    )
    loads.start(span_at(order, 0))
    state.start(0)
    state.wait(0)
    for i in range(1, SPANS):
        loads.start(span_at(order, i))
    for c in range(1, SPANS):
        state.start(c)

    def one_span(c, carry):
        count = order[c] + 1

        @pl.when(c > 0)
        def _():
            state.wait(c)

        block = Block(q2, l.at[c], acc.at[c])
        block.load(q_s[c])
        over_spans(order, c, loads, block, k_s, v_s)

        @pl.when(block.finish(o_s.at[c]))
        def _():
            block.clear()
            m[...] = jnp.full(m.shape, LOW, jnp.float32)

            def fetch(k, v):
                piece = Loads(lambda _: [(k, k_x), (v, v_x)], x_sems)
                piece.start(0)
                piece.wait(0)

            def careful_step(i, carry):
                span = span_at(order, i)
                for kv in spans:
                    fetch(kv.at[0, span], kv.at[1, span])
                    block.careful(m, k_x[...], v_x[...])
                return carry

            lax.fori_loop(0, count, careful_step, 0)
            seen = blocks_seen(group, mask, c)
            for x in range(SPANS):
                held, chip = (here, there)[x // 2], x % 2
                fetch(held.at[2 * chip], held.at[2 * chip + 1])
                for b in range(2):

                    @pl.when(seen[2 * x + b] > 0)
                    def _():
                        rows = slice(b * BLK, (b + 1) * BLK)
                        block.careful(m, k_x[rows, :], v_x[rows, :])

            block.finish(o_s.at[c])

        results.start(c)
        return carry

    lax.fori_loop(0, SPANS, one_span, 0)
    for c in range(SPANS):
        results.wait(c)


def call(kernel, name, scalars, arrays, outs, out_space, scratch, flops):
    return pl.pallas_call(
        kernel,
        grid_spec=pltpu.PrefetchScalarGridSpec(
            num_scalar_prefetch=len(scalars),
            grid=(),
            in_specs=[pl.BlockSpec(memory_space=pl.ANY)] * len(arrays),
            out_specs=[pl.BlockSpec(memory_space=out_space)] * len(outs),
            scratch_shapes=[pltpu.VMEM((ROWS, 2 * HD), jnp.bfloat16)] + scratch,
        ),
        out_shape=[jax.ShapeDtypeStruct((SPANS, ROWS, HD), dtype) for dtype in outs],
        compiler_params=pltpu.CompilerParams(vmem_limit_bytes=MEMORY),
        cost_estimate=pl.CostEstimate(
            flops=flops, bytes_accessed=12_000_000, transcendentals=20_000_000
        ),
        name=name,
    )(*scalars, *arrays)


def sems(*shape):
    return pltpu.SemaphoreType.DMA(shape)


STATE = [pltpu.VMEM((SPANS, ROWS, HD), jnp.float32)] * 2
QUERIES = [pltpu.VMEM((SPANS, ROWS, HD), jnp.bfloat16)]
SPAN_KEYS = [pltpu.VMEM((SPANS, 2 * ROWS, HD), jnp.bfloat16)] * 2
CACHE_KEYS = [pltpu.VMEM((SPAN_TOK, HD), jnp.bfloat16)] * 2
CAREFUL = [pltpu.VMEM((ROWS, HD), jnp.float32)] + [pltpu.VMEM((ROWS, HD), jnp.bfloat16)] * 2


def near(group, order, mask, q, spans, cached):
    return call(
        near_kernel, "near", [group, order, mask], [q, *spans, *cached],
        [jnp.float32] * 2, pl.ANY,
        STATE + QUERIES + SPAN_KEYS + CACHE_KEYS
        + [sems(SPANS, 1), sems(SPANS, 4), sems(SPANS, 2), sems(SPANS, 2)],
        29_000_000_000,
    )


def far(group, order, mask, q, spans, cached, state):
    return call(
        far_kernel, "far", [group, order, mask], [q, *spans, *cached, *state],
        [jnp.bfloat16], pl.ANY,
        STATE + QUERIES + SPAN_KEYS + [sems(SPANS, 4), sems(SPANS, 3)]
        + CAREFUL + [sems(1, 2)] + QUERIES + [sems(SPANS, 1)],
        17_000_000_000,
    )[0]


def on_device(
    queries, keys, values, cache_keys, cache_values, gate_table, noise_steps, span_order, block_mask
):
    group = jnp.reshape(lax.axis_index("span"), (1,)).astype(jnp.int32)
    apart = [lax.ppermute(x, "span", CHIP_SWAP) for x in (cache_keys, cache_values)]
    sent = pack(keys, values, queries).reshape(SPANS * H, 3 * PART, HD)
    got = lax.all_to_all(sent, EVERYONE, 0, 0, tiled=True)
    got, apart = lax.optimization_barrier((got, apart))
    cached = jnp.stack([cache_keys, cache_values, *apart])
    cached = [cached, lax.ppermute(cached, "span", CORE_SWAP)]
    kv0 = got[:, : 2 * PART].reshape(SPANS, H, 2, PART, HD).transpose(2, 0, 1, 3, 4)
    kv0 = kv0.reshape(2, SPANS, ROWS, HD)
    kv2 = lax.ppermute(kv0, "span", CHIP_SWAP)
    kv1 = lax.ppermute(kv0, "span", CORE_SWAP)
    got, kv1 = lax.optimization_barrier((got, kv1))
    q = got[:, 2 * PART :].reshape(SPANS, ROWS, HD)

    state = near(group, span_order, block_mask, q, [kv0, kv1], cached)
    kv2, state = lax.optimization_barrier((kv2, state))
    kv3 = lax.ppermute(kv2, "span", CORE_SWAP)
    out = far(group, span_order, block_mask, q, [kv0, kv1, kv2, kv3], cached, state)
    out = lax.all_to_all(out.reshape(SPANS * H, PART, HD), EVERYONE, 0, 0, tiled=True)
    return apply_gate(group, noise_steps, out.reshape(SPANS, H, PART, HD), gate_table)


def solution(mesh):
    placed = (
        P("span", "cp", None),
        P("span", "cp", None),
        P("span", "cp", None),
        P("span", "cp"),
        P("span", "cp"),
        P(),
        P(),
        P(),
        P(),
    )
    return jax.shard_map(
        on_device, mesh=mesh, in_specs=placed, out_specs=P("span", "cp", None), check_vma=False
    )
```
